32 devices in a mesh: batch: 8 (over z, x), blk: 4 (over y, core).
Axes of the slice: x: 2, y: 2, z: 4, core: 2. Of those that a mesh axis runs over, the one named last changes fastest.
Arguments:
- tokens: bfloat16 [8, 512, 2048], P('batch', 'blk'), may hold values from -6 to 6
- lengths: int32 [8, 4], P('batch'), may hold values from 0 to 512, as said below
- ln1_gain: bfloat16 [2048], P(('batch', 'blk')), may hold values from 0.5 to 1.5
- w_query: bfloat16 [2048, 2048], P(('batch', 'blk')), may hold values from -0.125 to 0.125
- w_key: bfloat16 [2048, 2048], P(('batch', 'blk')), may hold values from -0.125 to 0.125
- w_value: bfloat16 [2048, 4096], P(('batch', 'blk')), may hold values from -0.125 to 0.125
- w_gate: bfloat16 [2048, 4096], P(('batch', 'blk')), may hold values from -0.125 to 0.125
- w_out: bfloat16 [4096, 2048], P(('batch', 'blk')), may hold values from -0.125 to 0.125
- ln2_gain: bfloat16 [2048], P(('batch', 'blk')), may hold values from 0.5 to 1.5
- w_up: bfloat16 [2048, 4096], P(('batch', 'blk')), may hold values from -0.125 to 0.125
- w_down: bfloat16 [4096, 2048], P(('batch', 'blk')), may hold values from -0.125 to 0.125
- cotangent: bfloat16 [8, 512, 2048], P('batch', 'blk'), may hold values from -6 to 6
Outputs:
- output: bfloat16 [8, 512, 2048], P('batch', 'blk')
- tokens_grad: float32 [8, 512, 2048], P('batch', 'blk')
- ln1_gain_grad: float32 [2048], P(('batch', 'blk'))
- w_query_grad: float32 [2048, 2048], P(('batch', 'blk'))
- w_key_grad: float32 [2048, 2048], P(('batch', 'blk'))
- w_value_grad: float32 [2048, 4096], P(('batch', 'blk'))
- w_gate_grad: float32 [2048, 4096], P(('batch', 'blk'))
- w_out_grad: float32 [4096, 2048], P(('batch', 'blk'))
- ln2_gain_grad: float32 [2048], P(('batch', 'blk'))
- w_up_grad: float32 [2048, 4096], P(('batch', 'blk'))
- w_down_grad: float32 [4096, 2048], P(('batch', 'blk'))
The draws below stay inside these ranges and needn't reach their ends.
Inputs may be any that keep to these rules, and one draw needn't show every extreme that they name: `lengths`: each row's four entries sum to 512. A row either holds one sequence of 512 tokens and no padding (its other entries 0; at least one row does), or three sequences of 128 tokens or more each, followed by fewer than 128 tokens of padding.
All inputs are finite; a program needn't handle non-finite values.
Results may differ from the reference program's by a relative error of at most 0.014.
Values may be sent and summed in bfloat16 or wider, within the bound.
No kernel may reach another device: no remote copies, remote signals or barrier semaphores. Data moves between devices by JAX's collectives and lax.ppermute only.
A program may use at most 576 MiB of HBM per device.

```python
import math
from functools import partial
import jax
import jax.numpy as jnp
from jax import lax

D = 2048
HEADS = 8
HK = 256
HV = 512
FF = 4096
TOK_DEV = 128
QK = 2048
VD = 4096
ROW = 512
ROWS = 8
N_BLK = 4


def draw_lengths(key, part):
    key_pad = jax.random.fold_in(key, 11)
    key_first = jax.random.fold_in(key, 23)
    key_second = jax.random.fold_in(key, 37)
    key_kind = jax.random.fold_in(key, 41)
    key_pick = jax.random.fold_in(key, 53)
    padding = jax.random.randint(key_pad, (ROWS,), 0, TOK_DEV, dtype=jnp.int32)
    avail = (ROW - padding).astype(jnp.int32)
    first = jax.random.randint(key_first, (ROWS,), TOK_DEV, avail - 2 * TOK_DEV + 1, dtype=jnp.int32)
    second = jax.random.randint(key_second, (ROWS,), TOK_DEV, avail - first - TOK_DEV + 1, dtype=jnp.int32)
    third = (avail - first - second).astype(jnp.int32)
    single = jax.random.randint(key_kind, (ROWS,), 0, 4, dtype=jnp.int32) == 0
    chosen = jax.random.randint(key_pick, (), 0, ROWS, dtype=jnp.int32)
    single = single | (jnp.arange(ROWS, dtype=jnp.int32) == chosen)
    first = jnp.where(single, ROW, first).astype(jnp.int32)
    second = jnp.where(single, 0, second).astype(jnp.int32)
    third = jnp.where(single, 0, third).astype(jnp.int32)
    padding = jnp.where(single, 0, padding).astype(jnp.int32)
    return jnp.stack([first, second, third, padding], axis=1).astype(jnp.int32)


def level_of(own_key, extent, shards, smallest, largest):
    level = 1.0
    for dim, shards_of in shards:
        draws = jax.random.uniform(jax.random.fold_in(jax.random.fold_in(own_key, 6), dim), (shards_of,), jnp.float32, smallest / len(shards), largest / len(shards))
        level = level * jnp.repeat(jnp.exp(draws), extent[dim] // shards_of).reshape((-1,) + (1,) * (len(extent) - 1 - dim))
    return level


def scatter_about(own_key, extent, scale, limit, shards=(), kind=jnp.bfloat16):
    level = level_of(own_key, extent, shards, -0.22, 0.18) if shards else 1.0
    array = jax.random.normal(own_key, extent, jnp.float32) * scale * level
    return jnp.minimum(jnp.maximum(array, -limit), limit).astype(kind)


def setup_inputs(seed: int = 0) -> dict:
    splits = jax.random.split(jax.random.key(seed), 13)
    return {
        "tokens": scatter_about(splits[0], (ROWS, ROW, D), 1.0, 6.0, ((0, 8), (1, 4))),
        "lengths": draw_lengths(jax.random.fold_in(splits[12], 71), 0),
        "ln1_gain": jnp.clip(1.0 + 0.1 * jax.random.normal(splits[2], (D,), jnp.float32), 0.5, 1.5).astype(jnp.bfloat16),
        "w_query": scatter_about(splits[3], (D, QK), D ** -0.5, 0.125, ((0, 32),)),
        "w_key": scatter_about(splits[4], (D, QK), D ** -0.5, 0.125, ((0, 32),)),
        "w_value": scatter_about(splits[5], (D, VD), D ** -0.5, 0.125, ((0, 32),)),
        "w_gate": scatter_about(splits[6], (D, VD), D ** -0.5, 0.125, ((0, 32),)),
        "w_out": scatter_about(splits[7], (VD, D), (VD // 2) ** -0.5, 0.125, ((0, 32),)),
        "ln2_gain": jnp.clip(1.0 + 0.1 * jax.random.normal(splits[8], (D,), jnp.float32), 0.5, 1.5).astype(jnp.bfloat16),
        "w_up": scatter_about(splits[9], (D, FF), D ** -0.5, 0.125, ((0, 32),)),
        "w_down": scatter_about(splits[10], (FF, D), (FF // 2) ** -0.5, 0.125, ((0, 32),)),
        "cotangent": scatter_about(splits[11], (ROWS, ROW, D), 1.0, 6.0, ((0, 8), (1, 4))),
    }


EPS = 1e-06
GN_EPS = 0.1
ROPE_BASE = 10000.0
DECAY_SCALE = 32.0
HIGH_PRECISION = lax.Precision.HIGHEST

@jax.custom_vjp
def low(v):
    return lax.optimization_barrier(v.astype(jnp.bfloat16)).astype(jnp.float32)

@jax.custom_vjp
def low_back(v):
    return v

def low_keep(v):
    return (low(v), None)

def low_pass(kept, grad):
    return (grad,)

def back_keep(v):
    return (v, None)

def back_low(kept, grad):
    return (low(grad),)
low.defvjp(low_keep, low_pass)
low_back.defvjp(back_keep, back_low)

def matmul(left, right):
    return jnp.dot(left, right, precision=HIGH_PRECISION, preferred_element_type=jnp.float32)

def layer_norm(values, gain):
    centered = values - lax.optimization_barrier(jnp.mean(values, axis=-1, keepdims=True))
    spread = lax.optimization_barrier(jnp.mean(centered * centered, axis=-1, keepdims=True))
    return centered * lax.rsqrt(spread + EPS) * gain

def group_gate(mixed, gate):
    centered = mixed - lax.optimization_barrier(jnp.mean(mixed, axis=-1, keepdims=True))
    spread = lax.optimization_barrier(jnp.mean(centered * centered, axis=-1, keepdims=True))
    normed = centered * lax.rsqrt(spread + GN_EPS)
    return normed.reshape(gate.shape) * jax.nn.silu(gate)

def gelu_exact(values):
    return jax.nn.gelu(values, approximate=False)

def rotary_tables(positions, half):
    expo = jnp.arange(half, dtype=jnp.float32) / (half - 1)
    freq = jnp.exp(-math.log(ROPE_BASE) * expo)
    angle = positions[:, None] * freq[None, :]
    return (jnp.cos(angle), jnp.sin(angle))

def rotate(values, cosine, sine):
    half = values.shape[-1] // 2
    front = values[..., :half]
    back = values[..., half:]
    cosine = cosine[:, None, :]
    sine = sine[:, None, :]
    return jnp.concatenate([front * cosine - back * sine, back * cosine + front * sine], axis=-1)

def block_step(carry, blockin, rates):
    state, seg_prev = carry
    block_queries, block_keys, block_values, segb, validb = blockin
    tlen = block_queries.shape[0]
    loc = jnp.arange(tlen, dtype=jnp.int32)
    gap = (loc[:, None] - loc[None, :]).astype(jnp.float32)
    allowed = (segb[:, None] == segb[None, :]) & (gap >= 0) & validb[:, None] & validb[None, :]
    decay = jnp.where(allowed[None], jnp.exp(-rates[:, None, None] * jnp.maximum(gap, 0.0)[None]), 0.0)
    score_matrix = low_back(jnp.einsum('svg,uvg->vsu', block_queries, block_keys, precision=HIGH_PRECISION))
    weights = low(score_matrix * decay)
    inner = jnp.einsum('hnm,mhe->nhe', weights, block_values, precision=HIGH_PRECISION)
    locf = loc.astype(jnp.float32)
    reads = ((segb == seg_prev) & validb).astype(jnp.float32)
    read_scale = jnp.exp(-(locf[:, None] + 1.0) * rates[None, :]) * reads[:, None]
    query_scaled = low(block_queries * read_scale[:, :, None])
    past = low(state)
    outer = jnp.einsum('nhd,hde->nhe', query_scaled, past, precision=HIGH_PRECISION)
    seg_last = segb[tlen - 1]
    writes = ((segb == seg_last) & validb).astype(jnp.float32)
    write_scale = jnp.exp(-(tlen - 1.0 - locf)[:, None] * rates[None, :]) * writes[:, None]
    scaled_key_rows = low(block_keys * write_scale[:, :, None])
    state_update = low_back(jnp.einsum('yzj,yzw->zjw', scaled_key_rows, block_values, precision=HIGH_PRECISION))
    carry_scale = jnp.exp(-tlen * rates) * (seg_last == seg_prev).astype(jnp.float32)
    new_state = carry_scale[:, None, None] * state + state_update
    return ((new_state, seg_last), inner + outer)

def layer_row(row_tokens, lens, gain_one, wq, wk, wv, wg, wo, gain_two, wu, wd):
    pos = jnp.arange(ROW, dtype=jnp.int32)
    first_cut = lens[0]
    second_cut = lens[0] + lens[1]
    third_cut = lens[0] + lens[1] + lens[2]
    seg = (pos >= first_cut).astype(jnp.int32) + (pos >= second_cut).astype(jnp.int32) + (pos >= third_cut).astype(jnp.int32)
    valid = seg < 3
    h1 = low(layer_norm(row_tokens, gain_one))
    query = low_back(matmul(h1, wq))
    key = low_back(matmul(h1, wk))
    value = low_back(matmul(h1, wv))
    gate = low_back(matmul(h1, wg))
    cosine, sine = rotary_tables(pos.astype(jnp.float32), HK // 2)
    rotated_queries = low(rotate(query.reshape(ROW, HEADS, HK), cosine, sine))
    rotated_keys = low(rotate(key.reshape(ROW, HEADS, HK), cosine, sine) * (1.0 / math.sqrt(HK)))
    head_values = low(value.reshape(ROW, HEADS, HV))
    rates = DECAY_SCALE * jnp.exp2(-jnp.arange(HEADS, dtype=jnp.float32)) / ROW
    blocks = (rotated_queries.reshape(N_BLK, TOK_DEV, HEADS, HK), rotated_keys.reshape(N_BLK, TOK_DEV, HEADS, HK), head_values.reshape(N_BLK, TOK_DEV, HEADS, HV), seg.reshape(N_BLK, TOK_DEV), valid.reshape(N_BLK, TOK_DEV))
    start = (jnp.zeros((HEADS, HK, HV), jnp.float32), jnp.int32(-1))
    _, mixed = lax.scan(jax.checkpoint(partial(block_step, rates=rates)), start, blocks)
    mixed = low_back(mixed.reshape(ROW, HEADS, HV))
    gated = low(group_gate(mixed, gate))
    residual = row_tokens + low_back(matmul(gated, wo))
    h2 = low(layer_norm(residual, gain_two))
    hidden = low_back(matmul(h2, wu))
    act = low(gelu_exact(hidden))
    return residual + matmul(act, wd)

def forward(x, gain_one, wq, wk, wv, wg, wo, gain_two, wu, wd, lengths):

    def one_row(item):
        row_tokens, lens = item
        return layer_row(row_tokens, lens, gain_one, wq, wk, wv, wg, wo, gain_two, wu, wd)
    return lax.map(jax.checkpoint(one_row), (x, lengths))

def reference(tokens, lengths, ln1_gain, w_query, w_key, w_value, w_gate, w_out, ln2_gain, w_up, w_down, cotangent):
    single_float = jnp.float32

    def whole(x, g1, wq, wk, wv, wg, wo, g2, wu, wd):
        return forward(x, g1, wq, wk, wv, wg, wo, g2, wu, wd, lengths)
    output, pullback = jax.vjp(whole, tokens.astype(single_float), ln1_gain.astype(single_float), w_query.astype(single_float), w_key.astype(single_float), w_value.astype(single_float), w_gate.astype(single_float), w_out.astype(single_float), ln2_gain.astype(single_float), w_up.astype(single_float), w_down.astype(single_float))
    grads = pullback(cotangent.astype(single_float))
    return (output.astype(jnp.bfloat16), grads[0], grads[1], grads[2], grads[3], grads[4], grads[5], grads[6], grads[7], grads[8], grads[9])
```

```python
import math

import jax
import jax.numpy as jnp
from jax import lax
from jax.sharding import Mesh, PartitionSpec as P

HEADS = 8
HK = 256
HV = 512
EPS = 1e-06
GN_EPS = 0.1
ROPE_BASE = 10000.0
DECAY_SCALE = 32.0

F32 = jnp.float32
BF16 = jnp.bfloat16
TP = ("x", "k")
ALL = ("z", "x", "k")


def dot(a, b):
    return jnp.dot(a, b, preferred_element_type=F32)


def dot_nt(a, b):
    return lax.dot_general(a, b, (((1,), (1,)), ((), ())), preferred_element_type=F32)


def dot_tn(a, b):
    return lax.dot_general(a, b, (((0,), (0,)), ((), ())), preferred_element_type=F32)


def group_gate(mixed, gate):
    centered = mixed - jnp.mean(mixed, axis=-1, keepdims=True)
    spread = jnp.mean(centered * centered, axis=-1, keepdims=True)
    normed = centered * lax.rsqrt(spread + GN_EPS)
    return normed * jax.nn.silu(gate)


def gelu_exact(values):
    return jax.nn.gelu(values, approximate=False)


def normed_rows(values):
    centered = values - jnp.mean(values, axis=-1, keepdims=True)
    scale = lax.rsqrt(jnp.mean(centered * centered, axis=-1, keepdims=True) + EPS)
    return centered * scale, scale


def norm_back(grads, normed, scale):
    shift = jnp.mean(grads, axis=-1, keepdims=True)
    along = jnp.mean(grads * normed, axis=-1, keepdims=True)
    return scale * (grads - shift - normed * along)


def along(own):
    return lax.all_gather(own, "z", axis=0, tiled=True)


def summed_along(parts):
    return lax.psum_scatter(parts.astype(BF16), "z", scatter_dimension=0, tiled=True)


def after(value, *others):
    return lax.optimization_barrier((value, *others))[0]


class Plane:
    def __init__(self):
        self.rows = lax.axis_size("x")
        self.blocks = lax.axis_size("k")
        self.size = self.rows * self.blocks
        self.fast = self.rows == 2 and self.blocks == 4
        if self.fast:
            self.order = lax.axis_index("k") ^ jnp.arange(4, dtype=jnp.int32)
        else:
            self.order = jnp.arange(self.blocks, dtype=jnp.int32)

    def swap(self, v, mask):
        return lax.ppermute(v, TP, [(j, j ^ mask) for j in range(self.size)])

    def lengths(self, own):
        if self.fast:
            return jnp.stack([own, self.swap(own, 4)])
        return lax.all_gather(own, "x", axis=0, tiled=False)

    def gather(self, own):
        if not self.fast:
            return lax.all_gather(own, TP, axis=0, tiled=True)
        held = {0: own}
        for mask in (6, 4, 2):
            held[mask] = self.swap(own, mask)
        for mask in (0, 4, 2, 6):
            held[mask ^ 1] = self.swap(held[mask], 1)
        return jnp.concatenate([held[m] for m in range(8)], axis=0)

    def scatter(self, product, left, *fill):
        if not self.fast:
            return lax.psum_scatter(
                product(left).astype(BF16), TP, scatter_dimension=0, tiled=True
            ).astype(F32)
        paired = left.reshape(4, 2, left.shape[0] // 8, left.shape[1])
        away = product(paired[:, 1].reshape(-1, left.shape[1])).astype(BF16)
        come = self.swap(away, 1)
        kept = product(paired[:, 0].reshape(-1, left.shape[1])) + come.astype(F32)
        kept = kept.reshape(4, left.shape[0] // 8, -1)
        total = after(kept[0], *fill) if fill else kept[0]
        for i in (3, 2, 1):
            total = total + self.swap(kept[i].astype(BF16), 2 * i).astype(F32)
        return total

    def out_moves(self, turn):
        return [(4 * x + k, 2 * (k ^ turn) + x) for x in range(2) for k in range(4)]

    def out_in(self, own):
        nz = lax.axis_size("z")
        if not (self.fast and nz == 4):
            pairs = [(j * nz + i, i * self.size + j) for i in range(nz) for j in range(self.size)]
            return along(lax.ppermute(own, ALL, pairs))
        whole = along(own)
        rows = own.shape[0]
        k, pair = lax.axis_index("k"), lax.axis_index(TP) // 2
        got = jnp.zeros_like(whole)
        for turn in range(4):
            part = lax.dynamic_slice_in_dim(whole, (k ^ turn) * rows, rows, 0)
            part = lax.ppermute(part, TP, self.out_moves(turn))
            got = lax.dynamic_update_slice_in_dim(got, part, (pair ^ turn) * rows, 0)
        return got

    def out_back(self, parts):
        nz = lax.axis_size("z")
        if not (self.fast and nz == 4):
            pairs = [(i * self.size + j, j * nz + i) for i in range(nz) for j in range(self.size)]
            return lax.ppermute(summed_along(parts), ALL, pairs)
        rows = parts.shape[0] // 4
        k, pair = lax.axis_index("k"), lax.axis_index(TP) // 2
        got = jnp.zeros_like(parts)
        for turn in range(4):
            part = lax.dynamic_slice_in_dim(parts, (pair ^ turn) * rows, rows, 0)
            part = lax.ppermute(part, TP, [(b, a) for a, b in self.out_moves(turn)])
            got = lax.dynamic_update_slice_in_dim(got, part, (k ^ turn) * rows, 0)
        return summed_along(got)

    def exchange(self, v):
        return lax.all_to_all(v, TP, 0, 0, tiled=True)


def rotate(values, cosine, sine):
    half = values.shape[-1] // 2
    front = values[..., :half]
    back = values[..., half:]
    return jnp.concatenate([front * cosine - back * sine, back * cosine + front * sine], axis=-1)


def unrotate(grads, cosine, sine):
    half = grads.shape[-1] // 2
    front = grads[..., :half]
    back = grads[..., half:]
    return jnp.concatenate([front * cosine + back * sine, back * cosine - front * sine], axis=-1)


def shards(
    tokens,
    lengths,
    ln1_gain,
    w_query,
    w_key,
    w_value,
    w_gate,
    w_out,
    ln2_gain,
    w_up,
    w_down,
    cotangent,
):
    plane = Plane()
    nz, np_ = lax.axis_size("z"), plane.size
    head = lax.axis_index(TP)
    nrow = plane.rows
    tok = tokens[0]
    tlen, dim = tok.shape
    row_len = tlen * plane.blocks
    width = w_query.shape[0]
    units = w_down.shape[0]

    gain_one = ln1_gain.astype(F32)[:, None]
    gain_two = ln2_gain.astype(F32)[:, None]

    def by_head(w):
        scaled = (w.astype(F32) * gain_one).astype(BF16)
        return scaled.reshape(width, np_, -1).transpose(1, 0, 2)

    up_scaled = (w_up.astype(F32) * gain_two).astype(BF16)
    up_send = up_scaled.reshape(width, nz, np_, units).transpose(2, 0, 1, 3).reshape(np_, width, -1)
    sent = [by_head(w) for w in (w_query, w_key, w_value, w_gate)] + [up_send]
    got = plane.exchange(jnp.concatenate(sent, axis=2)).reshape(np_ * width, -1)
    cut = 2 * HK + HV
    w_o = plane.out_in(w_out)
    w_qkv = along(got[:, :cut])
    w_g = along(got[:, cut : cut + HV])
    w_u = along(got[:, cut + HV :])
    w_d = along(after(w_down, w_g))

    loc = jnp.arange(tlen, dtype=jnp.int32)
    pos = (plane.order[:, None] * tlen + loc[None, :]).reshape(-1)
    lens = plane.lengths(lengths[0])
    cut, seg = 0, 0
    for i in range(3):
        cut = cut + lens[:, i : i + 1]
        seg = seg + (pos[None, :] >= cut).astype(jnp.int32)
    valid = seg < 3
    rate = DECAY_SCALE * jnp.exp2(-head.astype(F32)) / row_len
    gap = (pos[:, None] - pos[None, :]).astype(F32)
    allowed = (seg[:, :, None] == seg[:, None, :]) & (gap >= 0)[None] & valid[:, :, None] & valid[:, None, :]
    decay = jnp.where(allowed, jnp.exp(-rate * jnp.maximum(gap, 0.0))[None], 0.0)
    half = HK // 2
    freq = jnp.exp(-math.log(ROPE_BASE) * (jnp.arange(half, dtype=F32) / (half - 1)))
    angle = pos.astype(F32)[:, None] * freq[None, :]
    cosine, sine = jnp.cos(angle)[None], jnp.sin(angle)[None]
    key_norm = 1.0 / math.sqrt(HK)

    xf = tok.astype(F32)
    hat1, scale1 = normed_rows(xf)
    h1 = plane.gather(hat1.astype(BF16))
    dy = plane.gather(after(cotangent[0], h1, got))
    heads = dot(after(h1, dy), w_qkv)
    qk = heads[:, : 2 * HK].reshape(nrow, row_len, 2 * HK)
    queries = rotate(qk[..., :HK], cosine, sine).astype(BF16)
    keys = (rotate(qk[..., HK:], cosine, sine) * key_norm).astype(BF16)
    values = heads[:, 2 * HK :].astype(BF16).reshape(nrow, row_len, HV)
    scores = jnp.einsum("rnd,rmd->rnm", queries, keys, preferred_element_type=F32)
    weights = (scores * decay).astype(BF16)
    mixed = jnp.einsum("rnm,rme->rne", weights, values, preferred_element_type=F32)
    gate = dot(h1, w_g)
    gated, gate_back = jax.vjp(group_gate, mixed.reshape(-1, HV), gate)
    gated = gated.astype(BF16)
    x2 = xf + plane.scatter(lambda a: dot(a, w_o), gated)

    hat2, scale2 = normed_rows(x2)
    h2 = plane.gather(hat2.astype(BF16))
    hidden, act_back = jax.vjp(gelu_exact, dot(h2, w_u))
    act = hidden.astype(BF16)

    down_parts = dot_tn(act, dy).astype(BF16)
    down_rows = summed_along(down_parts)
    d_hidden = act_back(dot_nt(dy, w_d))[0].astype(BF16)
    d_hidden = after(d_hidden, down_parts)
    up_parts = dot_tn(h2, d_hidden).astype(BF16)
    t2 = plane.scatter(lambda a: dot_nt(a, w_u), d_hidden, up_parts)
    up_rows = summed_along(up_parts)
    d_x2 = cotangent[0].astype(F32) + norm_back(t2, hat2, scale2)
    d_branch = plane.gather(after(d_x2.astype(BF16), down_rows))

    d_mixed, d_gate = gate_back(dot_nt(d_branch, w_o))
    d_gate = d_gate.astype(BF16)
    out_rows = plane.out_back(dot_tn(gated, d_branch).astype(BF16))
    d_mixed = d_mixed.astype(BF16).reshape(nrow, row_len, HV)
    d_values = jnp.einsum("rnm,rne->rme", weights, d_mixed, preferred_element_type=F32)
    d_values = d_values.astype(BF16).reshape(-1, HV)
    d_scores = jnp.einsum("rne,rme->rnm", d_mixed, values, preferred_element_type=F32)
    d_scores = (d_scores * decay).astype(BF16)
    d_query = jnp.einsum("rnm,rmd->rnd", d_scores, keys, preferred_element_type=F32)
    d_key = jnp.einsum("rnm,rnd->rmd", d_scores, queries, preferred_element_type=F32)
    d_query = unrotate(d_query, cosine, sine).astype(BF16)
    d_key = (unrotate(d_key, cosine, sine) * key_norm).astype(BF16)
    d_qk = jnp.concatenate([d_query, d_key], axis=-1).reshape(-1, 2 * HK)
    d_vg = after(jnp.concatenate([d_values, d_gate], axis=1), up_rows)
    vg_rows = summed_along(dot_tn(h1, d_vg))
    qk_rows = summed_along(dot_tn(h1, d_qk))
    qkv_cut = 2 * HK + HV
    d_heads = jnp.concatenate([d_qk, d_vg], axis=1)
    u1 = plane.scatter(
        lambda a: dot_nt(a[:, :qkv_cut], w_qkv) + dot_nt(a[:, qkv_cut:], w_g), after(d_heads, out_rows)
    )
    tokens_grad = d_x2 + norm_back(u1, hat1, scale1)
    output = x2 + plane.scatter(lambda a: dot(a, w_d), after(act, tokens_grad))

    out_grad = out_rows.astype(F32)

    def by_rows(rows):
        return plane.exchange(rows.reshape(np_, width, -1)).astype(F32).transpose(1, 0, 2)

    up_sum = by_rows(up_rows).reshape(width, np_, nz, units).transpose(0, 2, 1, 3).reshape(width, -1)
    vg_sum = by_rows(vg_rows)
    v_sum = vg_sum[:, :, :HV].reshape(width, -1)
    g_sum = vg_sum[:, :, HV:].reshape(width, -1)
    qk_sum = by_rows(after(qk_rows, output))
    q_sum = qk_sum[:, :, :HK].reshape(width, -1)
    k_sum = qk_sum[:, :, HK:].reshape(width, -1)

    def gain_sum(pairs):
        return sum(jnp.sum(w.astype(F32) * g, axis=1) for w, g in pairs)

    gain1_grad = gain_sum([(w_query, q_sum), (w_key, k_sum), (w_value, v_sum), (w_gate, g_sum)])
    gain2_grad = gain_sum([(w_up, up_sum)])
    return (
        output.astype(BF16)[None],
        tokens_grad[None],
        gain1_grad,
        q_sum * gain_one,
        k_sum * gain_one,
        v_sum * gain_one,
        g_sum * gain_one,
        out_grad,
        gain2_grad,
        up_sum * gain_two,
        down_rows.astype(F32),
    )


def solution(mesh):
    batch, blocks = mesh.shape["batch"], mesh.shape["blk"]
    rows = HEADS // blocks
    split = Mesh(mesh.devices.reshape(batch // rows, rows, blocks), ALL)
    by_token = P(("z", "x"), "k", None)
    by_row = P(ALL, None)
    by_one = P(ALL)
    return jax.shard_map(
        shards,
        mesh=split,
        in_specs=(
            by_token,
            P(("z", "x"), None),
            by_one,
            by_row,
            by_row,
            by_row,
            by_row,
            by_row,
            by_one,
            by_row,
            by_row,
            by_token,
        ),
        out_specs=(
            by_token,
            by_token,
            by_one,
            by_row,
            by_row,
            by_row,
            by_row,
            by_row,
            by_one,
            by_row,
            by_row,
        ),
        check_vma=False,
    )
```

```python
import math

import jax
import jax.numpy as jnp
from jax import lax
from jax.sharding import Mesh, PartitionSpec as P

HEADS = 8
HK = 256
HV = 512
EPS = 1e-06
GN_EPS = 0.1
ROPE_BASE = 10000.0
DECAY_SCALE = 32.0

F32 = jnp.float32
BF16 = jnp.bfloat16
TP = ("x", "k")
ALL = ("z", "x", "k")


def dot(a, b):
    return jnp.dot(a, b, preferred_element_type=F32)


def dot_nt(a, b):
    return lax.dot_general(a, b, (((1,), (1,)), ((), ())), preferred_element_type=F32)


def dot_tn(a, b):
    return lax.dot_general(a, b, (((0,), (0,)), ((), ())), preferred_element_type=F32)


def gelu_and_slope(values):
    below = 0.5 + 0.5 * lax.erf(values * math.sqrt(0.5))
    density = jnp.exp(-0.5 * values * values) * (1.0 / math.sqrt(2.0 * math.pi))
    return (values * below).astype(BF16), below + values * density


def normed_rows(values):
    centered = values - jnp.mean(values, axis=-1, keepdims=True)
    scale = lax.rsqrt(jnp.mean(centered * centered, axis=-1, keepdims=True) + EPS)
    return centered * scale, scale


def norm_back(grads, normed, scale):
    shift = jnp.mean(grads, axis=-1, keepdims=True)
    along = jnp.mean(grads * normed, axis=-1, keepdims=True)
    return scale * (grads - shift - normed * along)


def along(own):
    return lax.all_gather(own, "z", axis=0, tiled=True)


def summed_along(parts):
    return lax.psum_scatter(parts.astype(BF16), "z", scatter_dimension=0, tiled=True)


def along_by_hops(own):
    me = lax.axis_index("z")

    def hop(v, *pairs):
        return lax.ppermute(v, "z", pairs)

    near = hop(own, (0, 1), (1, 0), (2, 3), (3, 2))
    mid = hop(own, (1, 2), (2, 1))
    far = hop(near, (1, 2), (2, 1))
    out_mid = hop(mid, (1, 0), (2, 3))
    out_far = hop(far, (1, 0), (2, 3))
    inside = (me == 1) | (me == 2)
    held = [own, near, jnp.where(inside, mid, out_mid), jnp.where(inside, far, out_far)]
    places = jnp.array([[0, 1, 2, 3], [1, 0, 2, 3], [3, 2, 0, 1], [3, 2, 1, 0]], jnp.int32)
    return jnp.concatenate(held, axis=0), lax.dynamic_index_in_dim(places, me, keepdims=False)


def after(value, *others):
    return lax.optimization_barrier((value, *others))[0]


class Plane:
    def __init__(self):
        self.rows = lax.axis_size("x")
        self.blocks = lax.axis_size("k")
        self.size = self.rows * self.blocks
        self.fast = self.rows == 2 and self.blocks == 4
        if self.fast:
            self.order = lax.axis_index("k") ^ jnp.arange(4, dtype=jnp.int32)
        else:
            self.order = jnp.arange(self.blocks, dtype=jnp.int32)

    def swap(self, v, mask):
        return lax.ppermute(v, TP, [(j, j ^ mask) for j in range(self.size)])

    def lengths(self, own):
        if self.fast:
            return jnp.stack([own, self.swap(own, 4)])
        return lax.all_gather(own, "x", axis=0, tiled=False)

    def gather(self, own):
        if not self.fast:
            return lax.all_gather(own, TP, axis=0, tiled=True)
        held = {0: own}
        for mask in (6, 4, 2):
            held[mask] = self.swap(own, mask)
        for mask in (0, 4, 2, 6):
            held[mask ^ 1] = self.swap(held[mask], 1)
        return jnp.concatenate([held[m] for m in range(8)], axis=0)

    def scatter(self, product, left, *fill):
        if not self.fast:
            return lax.psum_scatter(
                product(left).astype(BF16), TP, scatter_dimension=0, tiled=True
            ).astype(F32)
        rows = left.shape[0] // 8
        blocks = [left[i * rows : (i + 1) * rows] for i in range(8)]
        come = {}
        for pair in ((6, 4), (2, 0)):
            away = product(jnp.concatenate([blocks[m ^ 1] for m in pair], axis=0)).astype(BF16)
            away = self.swap(away, 1)
            for i, m in enumerate(pair):
                come[m] = away[i * rows : (i + 1) * rows]
        sent = [
            self.swap((product(blocks[m]) + come[m].astype(F32)).astype(BF16), m) for m in (6, 4, 2)
        ]
        total = product(blocks[0]) + come[0].astype(F32)
        total = after(total, *fill) if fill else total
        for part in sent:
            total = total + part.astype(F32)
        return total

    def gather_parts(self, own):
        if not self.fast:
            whole = self.gather(own)
            return [whole], whole
        held = {0: own}
        for mask in (6, 4, 2):
            held[mask] = self.swap(own, mask)
        for mask in (0, 4, 2, 6):
            held[mask ^ 1] = self.swap(held[mask], 1)
        parts = [jnp.concatenate([held[m], held[m + 1]], axis=0) for m in (0, 4, 2, 6)]
        return parts, self.joined(parts)

    def joined(self, parts):
        if not self.fast:
            return parts[0]
        return jnp.concatenate([parts[i] for i in (0, 2, 1, 3)], axis=0)

    def parts_of(self, *arrays):
        if not self.fast:
            return [arrays]
        rows = arrays[0].shape[0] // 4
        return [[a[i * rows : (i + 1) * rows] for a in arrays] for i in (0, 2, 1, 3)]

    def out_moves(self, turn):
        return [(4 * x + k, 2 * (k ^ turn) + x) for x in range(2) for k in range(4)]

    def out_in(self, own, first):
        nz = lax.axis_size("z")
        if not (self.fast and nz == 4):
            pairs = [(j * nz + i, i * self.size + j) for i in range(nz) for j in range(self.size)]
            return along(lax.ppermute(own, ALL, pairs))
        whole = after(along(own), first)
        rows = own.shape[0]
        k, pair = lax.axis_index("k"), lax.axis_index(TP) // 2
        got = jnp.zeros_like(whole)
        for turn in range(4):
            part = lax.dynamic_slice_in_dim(whole, (k ^ turn) * rows, rows, 0)
            part = lax.ppermute(part, TP, self.out_moves(turn))
            got = lax.dynamic_update_slice_in_dim(got, part, (pair ^ turn) * rows, 0)
        return got

    def out_back(self, parts, last):
        nz = lax.axis_size("z")
        if not (self.fast and nz == 4):
            pairs = [(i * self.size + j, j * nz + i) for i in range(nz) for j in range(self.size)]
            return lax.ppermute(summed_along(parts), ALL, pairs)
        rows = parts.shape[0] // 4
        k, pair = lax.axis_index("k"), lax.axis_index(TP) // 2
        got = jnp.zeros_like(parts)
        for turn in range(4):
            part = lax.dynamic_slice_in_dim(parts, (pair ^ turn) * rows, rows, 0)
            part = lax.ppermute(part, TP, [(b, a) for a, b in self.out_moves(turn)])
            got = lax.dynamic_update_slice_in_dim(got, part, (k ^ turn) * rows, 0)
        return summed_along(after(got, last))

    def exchange(self, v):
        return lax.all_to_all(v, TP, 0, 0, tiled=True)


def rotate(values, cosine, sine):
    half = values.shape[-1] // 2
    front = values[..., :half]
    back = values[..., half:]
    return jnp.concatenate([front * cosine - back * sine, back * cosine + front * sine], axis=-1)


def unrotate(grads, cosine, sine):
    half = grads.shape[-1] // 2
    front = grads[..., :half]
    back = grads[..., half:]
    return jnp.concatenate([front * cosine + back * sine, back * cosine - front * sine], axis=-1)


def shards(
    tokens,
    lengths,
    ln1_gain,
    w_query,
    w_key,
    w_value,
    w_gate,
    w_out,
    ln2_gain,
    w_up,
    w_down,
    cotangent,
):
    plane = Plane()
    nz, np_ = lax.axis_size("z"), plane.size
    head = lax.axis_index(TP)
    nrow = plane.rows
    tok = tokens[0]
    tlen, dim = tok.shape
    row_len = tlen * plane.blocks
    width = w_query.shape[0]
    units = w_down.shape[0]

    gain_one = ln1_gain.astype(F32)[:, None]
    gain_two = ln2_gain.astype(F32)[:, None]

    def by_head(w):
        scaled = (w.astype(F32) * gain_one).astype(BF16)
        return scaled.reshape(width, np_, -1).transpose(1, 0, 2)

    up_scaled = (w_up.astype(F32) * gain_two).astype(BF16)
    up_send = up_scaled.reshape(width, nz, np_, units).transpose(2, 0, 1, 3).reshape(np_, width, -1)
    cut = 2 * HK + HV
    sent = [by_head(w) for w in (w_query, w_key, w_value, w_gate)] + [up_send]
    got = plane.exchange(jnp.concatenate(sent, axis=2)).reshape(np_ * width, -1)
    w_h = along(got[:, : cut + HV])
    w_u = along(got[:, cut + HV :])
    w_d = along(after(w_down, w_h))

    loc = jnp.arange(tlen, dtype=jnp.int32)
    pos = (plane.order[:, None] * tlen + loc[None, :]).reshape(-1)
    lens = plane.lengths(lengths[0])
    edge, seg = 0, 0
    for i in range(3):
        edge = edge + lens[:, i : i + 1]
        seg = seg + (pos[None, :] >= edge).astype(jnp.int32)
    valid = seg < 3
    rate = DECAY_SCALE * jnp.exp2(-head.astype(F32)) / row_len
    gap = (pos[:, None] - pos[None, :]).astype(F32)
    allowed = (seg[:, :, None] == seg[:, None, :]) & (gap >= 0)[None] & valid[:, :, None] & valid[:, None, :]
    decay = jnp.where(allowed, jnp.exp(-rate * jnp.maximum(gap, 0.0))[None], 0.0)
    half = HK // 2
    freq = jnp.exp(-math.log(ROPE_BASE) * (jnp.arange(half, dtype=F32) / (half - 1)))
    angle = pos.astype(F32)[:, None] * freq[None, :]
    cosine, sine = jnp.cos(angle)[None], jnp.sin(angle)[None]
    key_norm = 1.0 / math.sqrt(HK)

    xf = tok.astype(F32)
    hat1, scale1 = normed_rows(xf)
    h1 = plane.gather(hat1.astype(BF16))
    dy = plane.gather(after(cotangent[0], h1, got))
    w_o = plane.out_in(w_out, dy)
    heads = dot(after(h1, dy), w_h)
    qk = heads[:, : 2 * HK].reshape(nrow, row_len, 2 * HK)
    queries = rotate(qk[..., :HK], cosine, sine).astype(BF16)
    keys = (rotate(qk[..., HK:], cosine, sine) * key_norm).astype(BF16)
    values = heads[:, 2 * HK : cut].astype(BF16).reshape(nrow, row_len, HV)
    gate = heads[:, cut:]
    scores = jnp.einsum("rnd,rmd->rnm", queries, keys, preferred_element_type=F32)
    weights = (scores * decay).astype(BF16)
    mixed = jnp.einsum("rnm,rme->rne", weights, values, preferred_element_type=F32).reshape(-1, HV)
    centered = mixed - jnp.mean(mixed, axis=-1, keepdims=True)
    group_scale = lax.rsqrt(jnp.mean(centered * centered, axis=-1, keepdims=True) + GN_EPS)
    normed = centered * group_scale
    sig = jax.nn.sigmoid(gate)
    swish = gate * sig
    gated = (normed * swish).astype(BF16)
    x2 = xf + plane.scatter(lambda a: dot(a, w_o), gated, w_u)

    hat2, scale2 = normed_rows(x2)
    h2_parts, h2 = plane.gather_parts(hat2.astype(BF16))
    acts, slopes = zip(*[gelu_and_slope(dot(a, w_u)) for a in h2_parts])
    act, slope = plane.joined(acts), plane.joined(slopes)
    act, slope = lax.optimization_barrier((act, slope))

    down_parts = dot_tn(act, dy).astype(BF16)
    down_rows = summed_along(down_parts)
    d_hidden = (dot_nt(dy, w_d) * slope).astype(BF16)
    d_hidden = after(d_hidden, down_parts)
    up_parts = dot_tn(h2, d_hidden).astype(BF16)
    t2 = plane.scatter(lambda a: dot_nt(a, w_u), d_hidden, up_parts)
    up_rows = summed_along(up_parts)
    d_x2 = cotangent[0].astype(F32) + norm_back(t2, hat2, scale2)
    d_branch_parts, d_branch = plane.gather_parts(after(d_x2.astype(BF16), down_rows))
    gate_slope = normed * sig * (1.0 + gate * (1.0 - sig))
    d_mixed, d_gate = [], []
    for part, at in zip(d_branch_parts, plane.parts_of(normed, swish, gate_slope, group_scale)):
        n_at, swish_at, slope_at, scale_at = at
        d_gated = dot_nt(part, w_o)
        d_gate.append((d_gated * slope_at).astype(BF16))
        d_mixed.append(norm_back(d_gated * swish_at, n_at, scale_at).astype(BF16))
    d_mixed, d_gate = plane.joined(d_mixed), plane.joined(d_gate)
    g_rows = summed_along(dot_tn(h1, d_gate))
    d_mixed = d_mixed.reshape(nrow, row_len, HV)
    d_values = jnp.einsum("rnm,rne->rme", weights, d_mixed, preferred_element_type=F32)
    d_values = d_values.astype(BF16).reshape(-1, HV)
    d_scores = jnp.einsum("rne,rme->rnm", d_mixed, values, preferred_element_type=F32)
    d_scores = (d_scores * decay).astype(BF16)
    d_query = jnp.einsum("rnm,rmd->rnd", d_scores, keys, preferred_element_type=F32)
    d_key = jnp.einsum("rnm,rnd->rmd", d_scores, queries, preferred_element_type=F32)
    d_query = unrotate(d_query, cosine, sine).astype(BF16)
    d_key = (unrotate(d_key, cosine, sine) * key_norm).astype(BF16)
    d_qkv = jnp.concatenate([d_query.reshape(-1, HK), d_key.reshape(-1, HK), d_values], axis=1)
    qkv_parts = dot_tn(h1, after(d_qkv, up_rows)).astype(BF16)
    qkv_rows = summed_along(qkv_parts)
    d_heads = jnp.concatenate([d_qkv, d_gate], axis=1)
    u1 = plane.scatter(
        lambda a: dot_nt(a, w_h), after(d_heads, up_rows)
    )
    tokens_grad = d_x2 + norm_back(u1, hat1, scale1)
    gated_last, _ = lax.optimization_barrier((gated, qkv_parts))
    out_rows = plane.out_back(dot_tn(gated_last, d_branch).astype(BF16), u1)
    output = x2 + plane.scatter(lambda a: dot(a, w_d), after(act, tokens_grad))

    out_grad = out_rows.astype(F32)

    def by_rows(rows):
        return plane.exchange(rows.reshape(np_, width, -1)).astype(F32).transpose(1, 0, 2)

    up_sum = by_rows(after(up_rows, tokens_grad)).reshape(width, np_, nz, units).transpose(0, 2, 1, 3).reshape(width, -1)
    g_sum = by_rows(after(g_rows, tokens_grad)).reshape(width, -1)
    qkv_sum = by_rows(after(qkv_rows, output))
    q_sum = qkv_sum[:, :, :HK].reshape(width, -1)
    k_sum = qkv_sum[:, :, HK : 2 * HK].reshape(width, -1)
    v_sum = qkv_sum[:, :, 2 * HK :].reshape(width, -1)

    def gain_sum(pairs):
        return sum(jnp.sum(w.astype(F32) * g, axis=1) for w, g in pairs)

    gain1_grad = gain_sum([(w_query, q_sum), (w_key, k_sum), (w_value, v_sum), (w_gate, g_sum)])
    gain2_grad = gain_sum([(w_up, up_sum)])
    return (
        output.astype(BF16)[None],
        tokens_grad[None],
        gain1_grad,
        q_sum * gain_one,
        k_sum * gain_one,
        v_sum * gain_one,
        g_sum * gain_one,
        out_grad,
        gain2_grad,
        up_sum * gain_two,
        down_rows.astype(F32),
    )


def solution(mesh):
    batch, blocks = mesh.shape["batch"], mesh.shape["blk"]
    rows = HEADS // blocks
    split = Mesh(mesh.devices.reshape(batch // rows, rows, blocks), ALL)
    by_token = P(("z", "x"), "k", None)
    by_row = P(ALL, None)
    by_one = P(ALL)
    return jax.shard_map(
        shards,
        mesh=split,
        in_specs=(
            by_token,
            P(("z", "x"), None),
            by_one,
            by_row,
            by_row,
            by_row,
            by_row,
            by_row,
            by_one,
            by_row,
            by_row,
            by_token,
        ),
        out_specs=(
            by_token,
            by_token,
            by_one,
            by_row,
            by_row,
            by_row,
            by_row,
            by_row,
            by_one,
            by_row,
            by_row,
        ),
        check_vma=False,
    )
```

```python
import math

import jax
import jax.numpy as jnp
from jax import lax
from jax.sharding import Mesh, PartitionSpec as P

HEADS = 8
HK = 256
HV = 512
EPS = 1e-06
GN_EPS = 0.1
ROPE_BASE = 10000.0
DECAY_SCALE = 32.0

F32 = jnp.float32
BF16 = jnp.bfloat16
TP = ("x", "k")
ALL = ("z", "x", "k")


def dot(a, b):
    return jnp.dot(a, b, preferred_element_type=F32)


def dot_nt(a, b):
    return lax.dot_general(a, b, (((1,), (1,)), ((), ())), preferred_element_type=F32)


def dot_tn(a, b):
    return lax.dot_general(a, b, (((0,), (0,)), ((), ())), preferred_element_type=F32)


def gelu_and_slope(values):
    below = 0.5 + 0.5 * lax.erf(values * math.sqrt(0.5))
    density = jnp.exp(-0.5 * values * values) * (1.0 / math.sqrt(2.0 * math.pi))
    return (values * below).astype(BF16), below + values * density


def normed_rows(values):
    centered = values - jnp.mean(values, axis=-1, keepdims=True)
    scale = lax.rsqrt(jnp.mean(centered * centered, axis=-1, keepdims=True) + EPS)
    return centered * scale, scale


def norm_back(grads, normed, scale):
    shift = jnp.mean(grads, axis=-1, keepdims=True)
    along = jnp.mean(grads * normed, axis=-1, keepdims=True)
    return scale * (grads - shift - normed * along)


def along(own):
    return lax.all_gather(own, "z", axis=0, tiled=True)


def summed_along(parts):
    return lax.psum_scatter(parts.astype(BF16), "z", scatter_dimension=0, tiled=True)


def along_by_hops(own):
    me = lax.axis_index("z")

    def hop(v, *pairs):
        return lax.ppermute(v, "z", pairs)

    near = hop(own, (0, 1), (1, 0), (2, 3), (3, 2))
    mid = hop(own, (1, 2), (2, 1))
    far = hop(near, (1, 2), (2, 1))
    out_mid = hop(mid, (1, 0), (2, 3))
    out_far = hop(far, (1, 0), (2, 3))
    inside = (me == 1) | (me == 2)
    held = [own, near, jnp.where(inside, mid, out_mid), jnp.where(inside, far, out_far)]
    places = jnp.array([[0, 1, 2, 3], [1, 0, 2, 3], [3, 2, 0, 1], [3, 2, 1, 0]], jnp.int32)
    places = lax.dynamic_index_in_dim(places, me, keepdims=False)
    held = jnp.concatenate(held, axis=0)
    rows = own.shape[0]
    return jnp.concatenate(
        [lax.dynamic_slice_in_dim(held, places[i] * rows, rows, 0) for i in range(4)], axis=0
    )


def after(value, *others):
    return lax.optimization_barrier((value, *others))[0]


class Plane:
    def __init__(self):
        self.rows = lax.axis_size("x")
        self.blocks = lax.axis_size("k")
        self.size = self.rows * self.blocks
        self.fast = self.rows == 2 and self.blocks == 4
        if self.fast:
            self.order = lax.axis_index("k") ^ jnp.arange(4, dtype=jnp.int32)
        else:
            self.order = jnp.arange(self.blocks, dtype=jnp.int32)

    def swap(self, v, mask):
        return lax.ppermute(v, TP, [(j, j ^ mask) for j in range(self.size)])

    def lengths(self, own):
        if self.fast:
            return jnp.stack([own, self.swap(own, 4)])
        return lax.all_gather(own, "x", axis=0, tiled=False)

    def gather(self, own):
        if not self.fast:
            return lax.all_gather(own, TP, axis=0, tiled=True)
        held = {0: own}
        for mask in (6, 4, 2):
            held[mask] = self.swap(own, mask)
        for mask in (0, 4, 2, 6):
            held[mask ^ 1] = self.swap(held[mask], 1)
        return jnp.concatenate([held[m] for m in range(8)], axis=0)

    def scatter(self, product, left, *fill, late=None):
        if not self.fast:
            total = lax.psum_scatter(
                product(left).astype(BF16), TP, scatter_dimension=0, tiled=True
            ).astype(F32)
            return total if late is None else (total, late[0](late[1]))
        rows = left.shape[0] // 8
        blocks = [left[i * rows : (i + 1) * rows] for i in range(8)]
        come = {}
        for pair in ((6, 4), (2, 0)):
            away = product(jnp.concatenate([blocks[m ^ 1] for m in pair], axis=0)).astype(BF16)
            away = self.swap(away, 1)
            for i, m in enumerate(pair):
                come[m] = away[i * rows : (i + 1) * rows]
        sums = [(product(blocks[m]) + come[m].astype(F32)).astype(BF16) for m in (6, 4, 2)]
        if late is not None:
            held = lax.optimization_barrier((*sums, *late[1]))
            sums, filled = held[:3], late[0](held[3:])
        sent = [self.swap(part, m) for part, m in zip(sums, (6, 4, 2))]
        total = product(blocks[0]) + come[0].astype(F32)
        if late is not None:
            total = after(total, filled)
        total = after(total, *fill) if fill else total
        for part in sent:
            total = total + part.astype(F32)
        return total if late is None else (total, filled)

    def gather_parts(self, own):
        if not self.fast:
            whole = self.gather(own)
            return [whole], [whole]
        held = {0: own}
        for mask in (6, 4, 2):
            held[mask] = self.swap(own, mask)
        for mask in (0, 4, 2, 6):
            held[mask ^ 1] = self.swap(held[mask], 1)
        parts = [jnp.concatenate([held[m], held[m + 1]], axis=0) for m in (0, 4, 2, 6)]
        return parts, [held[m] for m in range(8)]

    def joined(self, parts):
        if not self.fast:
            return parts[0]
        return jnp.concatenate([parts[i] for i in (0, 2, 1, 3)], axis=0)

    def parts_of(self, *arrays):
        if not self.fast:
            return [arrays]
        rows = arrays[0].shape[0] // 4
        return [[a[i * rows : (i + 1) * rows] for a in arrays] for i in (0, 2, 1, 3)]

    def out_moves(self, turn):
        return [(4 * x + k, 2 * (k ^ turn) + x) for x in range(2) for k in range(4)]

    def out_along(self, own):
        return along_by_hops(own) if self.fast and lax.axis_size("z") == 4 else own

    def out_in(self, own, first):
        nz = lax.axis_size("z")
        if not (self.fast and nz == 4):
            pairs = [(j * nz + i, i * self.size + j) for i in range(nz) for j in range(self.size)]
            return along(lax.ppermute(own, ALL, pairs))
        whole = after(own, first)
        rows = own.shape[0] // 4
        k, pair = lax.axis_index("k"), lax.axis_index(TP) // 2
        got = jnp.zeros_like(whole)
        for turn in range(4):
            part = lax.dynamic_slice_in_dim(whole, (k ^ turn) * rows, rows, 0)
            part = lax.ppermute(part, TP, self.out_moves(turn))
            got = lax.dynamic_update_slice_in_dim(got, part, (pair ^ turn) * rows, 0)
        return got

    def out_back(self, parts, last):
        nz = lax.axis_size("z")
        if not (self.fast and nz == 4):
            pairs = [(i * self.size + j, j * nz + i) for i in range(nz) for j in range(self.size)]
            return lax.ppermute(summed_along(parts), ALL, pairs)
        rows = parts.shape[0] // 4
        k, pair = lax.axis_index("k"), lax.axis_index(TP) // 2
        got = jnp.zeros_like(parts)
        for turn in range(4):
            part = lax.dynamic_slice_in_dim(parts, (pair ^ turn) * rows, rows, 0)
            part = lax.ppermute(part, TP, [(b, a) for a, b in self.out_moves(turn)])
            got = lax.dynamic_update_slice_in_dim(got, part, (k ^ turn) * rows, 0)
        return summed_along(after(got, last))

    def exchange(self, v):
        return lax.all_to_all(v, TP, 0, 0, tiled=True)


def rotate(values, cosine, sine):
    half = values.shape[-1] // 2
    front = values[..., :half]
    back = values[..., half:]
    return jnp.concatenate([front * cosine - back * sine, back * cosine + front * sine], axis=-1)


def unrotate(grads, cosine, sine):
    half = grads.shape[-1] // 2
    front = grads[..., :half]
    back = grads[..., half:]
    return jnp.concatenate([front * cosine + back * sine, back * cosine - front * sine], axis=-1)


def shards(
    tokens,
    lengths,
    ln1_gain,
    w_query,
    w_key,
    w_value,
    w_gate,
    w_out,
    ln2_gain,
    w_up,
    w_down,
    cotangent,
):
    plane = Plane()
    nz, np_ = lax.axis_size("z"), plane.size
    head = lax.axis_index(TP)
    nrow = plane.rows
    tok = tokens[0]
    tlen, dim = tok.shape
    row_len = tlen * plane.blocks
    width = w_query.shape[0]
    units = w_down.shape[0]

    gain_one = ln1_gain.astype(F32)[:, None]
    gain_two = ln2_gain.astype(F32)[:, None]

    def by_head(w):
        scaled = (w.astype(F32) * gain_one).astype(BF16)
        return scaled.reshape(width, np_, -1).transpose(1, 0, 2)

    up_scaled = (w_up.astype(F32) * gain_two).astype(BF16)
    up_send = up_scaled.reshape(width, nz, np_, units).transpose(2, 0, 1, 3).reshape(np_, width, -1)
    cut = 2 * HK + HV
    sent = [by_head(w) for w in (w_query, w_key, w_value, w_gate)]
    out_held = plane.out_along(w_out)
    got = plane.exchange(jnp.concatenate(sent, axis=2)).reshape(np_ * width, -1)
    w_h = along(after(got, out_held))
    up_got = plane.exchange(after(up_send, got)).reshape(np_ * width, -1)
    w_u = along(up_got)
    w_d = along(after(w_down, w_h))

    loc = jnp.arange(tlen, dtype=jnp.int32)
    pos = (plane.order[:, None] * tlen + loc[None, :]).reshape(-1)
    lens = plane.lengths(lengths[0])
    edge, seg = 0, 0
    for i in range(3):
        edge = edge + lens[:, i : i + 1]
        seg = seg + (pos[None, :] >= edge).astype(jnp.int32)
    valid = seg < 3
    rate = DECAY_SCALE * jnp.exp2(-head.astype(F32)) / row_len
    gap = (pos[:, None] - pos[None, :]).astype(F32)
    allowed = (seg[:, :, None] == seg[:, None, :]) & (gap >= 0)[None] & valid[:, :, None] & valid[:, None, :]
    decay = jnp.where(allowed, jnp.exp(-rate * jnp.maximum(gap, 0.0))[None], 0.0)
    half = HK // 2
    freq = jnp.exp(-math.log(ROPE_BASE) * (jnp.arange(half, dtype=F32) / (half - 1)))
    angle = pos.astype(F32)[:, None] * freq[None, :]
    cosine, sine = jnp.cos(angle)[None], jnp.sin(angle)[None]
    key_norm = 1.0 / math.sqrt(HK)

    xf = tok.astype(F32)
    hat1, scale1 = normed_rows(xf)
    h1 = plane.gather(after(hat1.astype(BF16), up_got))
    dy = plane.gather(after(cotangent[0], h1, got))
    w_o = plane.out_in(out_held, dy)
    heads = dot(after(h1, dy), w_h)
    qk = heads[:, : 2 * HK].reshape(nrow, row_len, 2 * HK)
    queries = rotate(qk[..., :HK], cosine, sine).astype(BF16)
    keys = (rotate(qk[..., HK:], cosine, sine) * key_norm).astype(BF16)
    values = heads[:, 2 * HK : cut].astype(BF16).reshape(nrow, row_len, HV)
    gate = heads[:, cut:]
    scores = jnp.einsum("rnd,rmd->rnm", queries, keys, preferred_element_type=F32)
    weights = (scores * decay).astype(BF16)
    mixed = jnp.einsum("rnm,rme->rne", weights, values, preferred_element_type=F32).reshape(-1, HV)
    centered = mixed - jnp.mean(mixed, axis=-1, keepdims=True)
    group_scale = lax.rsqrt(jnp.mean(centered * centered, axis=-1, keepdims=True) + GN_EPS)
    normed = centered * group_scale
    sig = jax.nn.sigmoid(gate)
    swish = gate * sig
    gated = (normed * swish).astype(BF16)
    x2 = xf + plane.scatter(lambda a: dot(a, w_o), gated, w_u)

    hat2, scale2 = normed_rows(x2)
    h2_parts, h2_blocks = plane.gather_parts(hat2.astype(BF16))
    acts, slopes = zip(*[gelu_and_slope(dot(a, w_u)) for a in h2_parts])
    act = plane.joined(acts)

    down_parts = dot_tn(act, dy).astype(BF16)
    down_rows = summed_along(down_parts)
    slope = plane.joined(lax.optimization_barrier((*slopes, down_parts))[:-1])
    d_hidden = (dot_nt(dy, w_d) * slope).astype(BF16)

    def up_product(held):
        return dot_tn(jnp.concatenate(held[:-1], axis=0), held[-1]).astype(BF16)

    t2, up_parts = plane.scatter(
        lambda a: dot_nt(a, w_u), d_hidden, late=(up_product, (*h2_blocks, d_hidden))
    )
    up_rows = summed_along(up_parts)
    d_x2 = cotangent[0].astype(F32) + norm_back(t2, hat2, scale2)
    d_branch_parts, d_branch_blocks = plane.gather_parts(after(d_x2.astype(BF16), down_rows))
    gate_slope = normed * sig * (1.0 + gate * (1.0 - sig))
    d_mixed, d_gate = [], []
    for part, at in zip(d_branch_parts, plane.parts_of(normed, swish, gate_slope, group_scale)):
        n_at, swish_at, slope_at, scale_at = at
        d_gated = dot_nt(part, w_o)
        d_gate.append((d_gated * slope_at).astype(BF16))
        d_mixed.append(norm_back(d_gated * swish_at, n_at, scale_at).astype(BF16))
    d_mixed, d_gate = plane.joined(d_mixed), plane.joined(d_gate)
    g_rows = summed_along(dot_tn(h1, d_gate))
    d_mixed = d_mixed.reshape(nrow, row_len, HV)
    d_values = jnp.einsum("rnm,rne->rme", weights, d_mixed, preferred_element_type=F32)
    d_values = d_values.astype(BF16).reshape(-1, HV)
    d_scores = jnp.einsum("rne,rme->rnm", d_mixed, values, preferred_element_type=F32)
    d_scores = (d_scores * decay).astype(BF16)
    d_query = jnp.einsum("rnm,rmd->rnd", d_scores, keys, preferred_element_type=F32)
    d_key = jnp.einsum("rnm,rnd->rmd", d_scores, queries, preferred_element_type=F32)
    d_query = unrotate(d_query, cosine, sine).astype(BF16)
    d_key = (unrotate(d_key, cosine, sine) * key_norm).astype(BF16)
    d_qkv = jnp.concatenate([d_query.reshape(-1, HK), d_key.reshape(-1, HK), d_values], axis=1)
    qkv_parts = dot_tn(h1, after(d_qkv, up_rows)).astype(BF16)
    qkv_rows = summed_along(qkv_parts)
    d_heads = jnp.concatenate([d_qkv, d_gate], axis=1)
    u1 = plane.scatter(
        lambda a: dot_nt(a, w_h), after(d_heads, up_rows)
    )
    tokens_grad = d_x2 + norm_back(u1, hat1, scale1)
    gated_last, *rest = lax.optimization_barrier((gated, *d_branch_blocks, qkv_parts))
    d_branch = jnp.concatenate(rest[:-1], axis=0)
    out_rows = plane.out_back(dot_tn(gated_last, d_branch).astype(BF16), u1)
    output = x2 + plane.scatter(lambda a: dot(a, w_d), after(act, tokens_grad))

    out_grad = out_rows.astype(F32)

    def by_rows(rows):
        return plane.exchange(rows.reshape(np_, width, -1)).astype(F32).transpose(1, 0, 2)

    up_sum = by_rows(after(up_rows, tokens_grad)).reshape(width, np_, nz, units).transpose(0, 2, 1, 3).reshape(width, -1)
    g_sum = by_rows(after(g_rows, tokens_grad)).reshape(width, -1)
    qkv_sum = by_rows(after(qkv_rows, output))
    q_sum = qkv_sum[:, :, :HK].reshape(width, -1)
    k_sum = qkv_sum[:, :, HK : 2 * HK].reshape(width, -1)
    v_sum = qkv_sum[:, :, 2 * HK :].reshape(width, -1)

    def gain_sum(pairs):
        return sum(jnp.sum(w.astype(F32) * g, axis=1) for w, g in pairs)

    gain1_grad = gain_sum([(w_query, q_sum), (w_key, k_sum), (w_value, v_sum), (w_gate, g_sum)])
    gain2_grad = gain_sum([(w_up, up_sum)])
    return (
        output.astype(BF16)[None],
        tokens_grad[None],
        gain1_grad,
        q_sum * gain_one,
        k_sum * gain_one,
        v_sum * gain_one,
        g_sum * gain_one,
        out_grad,
        gain2_grad,
        up_sum * gain_two,
        down_rows.astype(F32),
    )


def solution(mesh):
    batch, blocks = mesh.shape["batch"], mesh.shape["blk"]
    rows = HEADS // blocks
    split = Mesh(mesh.devices.reshape(batch // rows, rows, blocks), ALL)
    by_token = P(("z", "x"), "k", None)
    by_row = P(ALL, None)
    by_one = P(ALL)
    return jax.shard_map(
        shards,
        mesh=split,
        in_specs=(
            by_token,
            P(("z", "x"), None),
            by_one,
            by_row,
            by_row,
            by_row,
            by_row,
            by_row,
            by_one,
            by_row,
            by_row,
            by_token,
        ),
        out_specs=(
            by_token,
            by_token,
            by_one,
            by_row,
            by_row,
            by_row,
            by_row,
            by_row,
            by_one,
            by_row,
            by_row,
        ),
        check_vma=False,
    )
```

```python
import math

import jax
import jax.numpy as jnp
from jax import lax
from jax.sharding import Mesh, PartitionSpec as P

HEADS = 8
HK = 256
HV = 512
EPS = 1e-06
GN_EPS = 0.1
ROPE_BASE = 10000.0
DECAY_SCALE = 32.0

F32 = jnp.float32
BF16 = jnp.bfloat16
TP = ("x", "k")
ALL = ("z", "x", "k")


def dot(a, b):
    return jnp.dot(a, b, preferred_element_type=F32)


def dot_nt(a, b):
    return lax.dot_general(a, b, (((1,), (1,)), ((), ())), preferred_element_type=F32)


def dot_tn(a, b):
    return lax.dot_general(a, b, (((0,), (0,)), ((), ())), preferred_element_type=F32)


def gelu_and_slope(values):
    below = 0.5 + 0.5 * lax.erf(values * math.sqrt(0.5))
    density = jnp.exp(-0.5 * values * values) * (1.0 / math.sqrt(2.0 * math.pi))
    return (values * below).astype(BF16), below + values * density


def normed_rows(values):
    centered = values - jnp.mean(values, axis=-1, keepdims=True)
    scale = lax.rsqrt(jnp.mean(centered * centered, axis=-1, keepdims=True) + EPS)
    return centered * scale, scale


def norm_back(grads, normed, scale):
    shift = jnp.mean(grads, axis=-1, keepdims=True)
    along = jnp.mean(grads * normed, axis=-1, keepdims=True)
    return scale * (grads - shift - normed * along)


def along(own):
    return lax.all_gather(own, "z", axis=0, tiled=True)


def summed_along(parts):
    return lax.psum_scatter(parts.astype(BF16), "z", scatter_dimension=0, tiled=True)


def along_by_hops(own):
    me = lax.axis_index("z")

    def hop(v, *pairs):
        return lax.ppermute(v, "z", pairs)

    near = hop(own, (0, 1), (1, 0), (2, 3), (3, 2))
    mid = hop(own, (1, 2), (2, 1))
    far = hop(near, (1, 2), (2, 1))
    out_mid = hop(mid, (1, 0), (2, 3))
    out_far = hop(far, (1, 0), (2, 3))
    inside = (me == 1) | (me == 2)
    held = [own, near, jnp.where(inside, mid, out_mid), jnp.where(inside, far, out_far)]
    places = jnp.array([[0, 1, 2, 3], [1, 0, 2, 3], [3, 2, 0, 1], [3, 2, 1, 0]], jnp.int32)
    places = lax.dynamic_index_in_dim(places, me, keepdims=False)
    held = jnp.concatenate(held, axis=0)
    rows = own.shape[0]
    return jnp.concatenate(
        [lax.dynamic_slice_in_dim(held, places[i] * rows, rows, 0) for i in range(4)], axis=0
    )


def after(value, *others):
    return lax.optimization_barrier((value, *others))[0]


class Plane:
    def __init__(self):
        self.rows = lax.axis_size("x")
        self.blocks = lax.axis_size("k")
        self.size = self.rows * self.blocks
        self.fast = self.rows == 2 and self.blocks == 4
        if self.fast:
            self.order = lax.axis_index("k") ^ jnp.arange(4, dtype=jnp.int32)
        else:
            self.order = jnp.arange(self.blocks, dtype=jnp.int32)

    def swap(self, v, mask):
        return lax.ppermute(v, TP, [(j, j ^ mask) for j in range(self.size)])

    def lengths(self, own):
        if self.fast:
            return jnp.stack([own, self.swap(own, 4)])
        return lax.all_gather(own, "x", axis=0, tiled=False)

    def gather(self, own):
        if not self.fast:
            return lax.all_gather(own, TP, axis=0, tiled=True)
        held = {0: own}
        for mask in (6, 4, 2):
            held[mask] = self.swap(own, mask)
        for mask in (0, 4, 2, 6):
            held[mask ^ 1] = self.swap(held[mask], 1)
        return jnp.concatenate([held[m] for m in range(8)], axis=0)

    def scatter(self, product, left, *fill, late=None):
        if not self.fast:
            total = lax.psum_scatter(
                product(left).astype(BF16), TP, scatter_dimension=0, tiled=True
            ).astype(F32)
            return total if late is None else (total, late[0](late[1]))
        rows = left.shape[0] // 8
        blocks = [left[i * rows : (i + 1) * rows] for i in range(8)]
        come = {}
        for pair in ((6,), (4,), (2,), (0,)):
            away = product(jnp.concatenate([blocks[m ^ 1] for m in pair], axis=0)).astype(BF16)
            away = self.swap(away, 1)
            for i, m in enumerate(pair):
                come[m] = away[i * rows : (i + 1) * rows]
        sums = [(product(blocks[m]) + come[m].astype(F32)).astype(BF16) for m in (6, 4, 2)]
        if late is not None:
            held = lax.optimization_barrier((*sums, *late[1]))
            sums, filled = held[:3], late[0](held[3:])
        sent = [self.swap(part, m) for part, m in zip(sums, (6, 4, 2))]
        total = product(blocks[0]) + come[0].astype(F32)
        if late is not None:
            total = after(total, filled)
        total = after(total, *fill) if fill else total
        for part in sent:
            total = total + part.astype(F32)
        return total if late is None else (total, filled)

    def gather_parts(self, own):
        if not self.fast:
            whole = self.gather(own)
            return [whole], [whole]
        held = {0: own, 4: self.swap(own, 4), 2: self.swap(own, 2)}
        half = own.shape[0] // 2
        by_y, by_x = self.swap(held[4][:half], 2), self.swap(held[2][half:], 4)
        held[6] = jnp.concatenate([by_y, by_x], axis=0)
        for mask in (0, 4, 2, 6):
            held[mask ^ 1] = self.swap(held[mask], 1)
        parts = [jnp.concatenate([held[m], held[m + 1]], axis=0) for m in (0, 4, 2, 6)]
        return parts, [held[m] for m in range(8)]

    def joined(self, parts):
        if not self.fast:
            return parts[0]
        return jnp.concatenate([parts[i] for i in (0, 2, 1, 3)], axis=0)

    def parts_of(self, *arrays):
        if not self.fast:
            return [arrays]
        rows = arrays[0].shape[0] // 4
        return [[a[i * rows : (i + 1) * rows] for a in arrays] for i in (0, 2, 1, 3)]

    def out_moves(self, turn):
        return [(4 * x + k, 2 * (k ^ turn) + x) for x in range(2) for k in range(4)]

    def out_along(self, own):
        return along_by_hops(own) if self.fast and lax.axis_size("z") == 4 else own

    def out_in(self, own, first):
        nz = lax.axis_size("z")
        if not (self.fast and nz == 4):
            pairs = [(j * nz + i, i * self.size + j) for i in range(nz) for j in range(self.size)]
            return along(lax.ppermute(own, ALL, pairs))
        whole = after(own, first)
        rows = own.shape[0] // 4
        k, pair = lax.axis_index("k"), lax.axis_index(TP) // 2
        got = jnp.zeros_like(whole)
        for turn in range(4):
            part = lax.dynamic_slice_in_dim(whole, (k ^ turn) * rows, rows, 0)
            part = lax.ppermute(part, TP, self.out_moves(turn))
            got = lax.dynamic_update_slice_in_dim(got, part, (pair ^ turn) * rows, 0)
        return got

    def out_back(self, parts, last):
        nz = lax.axis_size("z")
        if not (self.fast and nz == 4):
            pairs = [(i * self.size + j, j * nz + i) for i in range(nz) for j in range(self.size)]
            return lax.ppermute(summed_along(parts), ALL, pairs)
        rows = parts.shape[0] // 4
        k, pair = lax.axis_index("k"), lax.axis_index(TP) // 2
        got = jnp.zeros_like(parts)
        for turn in range(4):
            part = lax.dynamic_slice_in_dim(parts, (pair ^ turn) * rows, rows, 0)
            part = lax.ppermute(part, TP, [(b, a) for a, b in self.out_moves(turn)])
            got = lax.dynamic_update_slice_in_dim(got, part, (k ^ turn) * rows, 0)
        return summed_along(after(got, last))

    def exchange(self, v):
        return lax.all_to_all(v, TP, 0, 0, tiled=True)


def rotate(values, cosine, sine):
    half = values.shape[-1] // 2
    front = values[..., :half]
    back = values[..., half:]
    return jnp.concatenate([front * cosine - back * sine, back * cosine + front * sine], axis=-1)


def unrotate(grads, cosine, sine):
    half = grads.shape[-1] // 2
    front = grads[..., :half]
    back = grads[..., half:]
    return jnp.concatenate([front * cosine + back * sine, back * cosine - front * sine], axis=-1)


def shards(
    tokens,
    lengths,
    ln1_gain,
    w_query,
    w_key,
    w_value,
    w_gate,
    w_out,
    ln2_gain,
    w_up,
    w_down,
    cotangent,
):
    plane = Plane()
    nz, np_ = lax.axis_size("z"), plane.size
    head = lax.axis_index(TP)
    nrow = plane.rows
    tok = tokens[0]
    tlen, dim = tok.shape
    row_len = tlen * plane.blocks
    width = w_query.shape[0]
    units = w_down.shape[0]

    gain_one = ln1_gain.astype(F32)[:, None]
    gain_two = ln2_gain.astype(F32)[:, None]

    def by_head(w):
        scaled = (w.astype(F32) * gain_one).astype(BF16)
        return scaled.reshape(width, np_, -1).transpose(1, 0, 2)

    up_scaled = (w_up.astype(F32) * gain_two).astype(BF16)
    up_send = up_scaled.reshape(width, nz, np_, units).transpose(2, 0, 1, 3).reshape(np_, width, -1)
    cut = 2 * HK + HV
    sent = [by_head(w) for w in (w_query, w_key, w_value, w_gate)]
    out_held = plane.out_along(w_out)
    got = plane.exchange(jnp.concatenate(sent, axis=2)).reshape(np_ * width, -1)
    w_h = along(after(got, out_held))
    up_got = plane.exchange(after(up_send, got)).reshape(np_ * width, -1)
    w_u = along(up_got)
    w_d = along(after(w_down, w_h))

    loc = jnp.arange(tlen, dtype=jnp.int32)
    pos = (plane.order[:, None] * tlen + loc[None, :]).reshape(-1)
    lens = plane.lengths(lengths[0])
    edge, seg = 0, 0
    for i in range(3):
        edge = edge + lens[:, i : i + 1]
        seg = seg + (pos[None, :] >= edge).astype(jnp.int32)
    valid = seg < 3
    rate = DECAY_SCALE * jnp.exp2(-head.astype(F32)) / row_len
    gap = (pos[:, None] - pos[None, :]).astype(F32)
    allowed = (seg[:, :, None] == seg[:, None, :]) & (gap >= 0)[None] & valid[:, :, None] & valid[:, None, :]
    decay = jnp.where(allowed, jnp.exp(-rate * jnp.maximum(gap, 0.0))[None], 0.0)
    half = HK // 2
    freq = jnp.exp(-math.log(ROPE_BASE) * (jnp.arange(half, dtype=F32) / (half - 1)))
    angle = pos.astype(F32)[:, None] * freq[None, :]
    cosine, sine = jnp.cos(angle)[None], jnp.sin(angle)[None]
    key_norm = 1.0 / math.sqrt(HK)

    xf = tok.astype(F32)
    hat1, scale1 = normed_rows(xf)
    h1 = plane.gather(after(hat1.astype(BF16), up_got))
    dy = plane.gather(after(cotangent[0], h1, got))
    w_o = plane.out_in(out_held, dy)
    heads = dot(after(h1, dy), w_h)
    qk = heads[:, : 2 * HK].reshape(nrow, row_len, 2 * HK)
    queries = rotate(qk[..., :HK], cosine, sine).astype(BF16)
    keys = (rotate(qk[..., HK:], cosine, sine) * key_norm).astype(BF16)
    values = heads[:, 2 * HK : cut].astype(BF16).reshape(nrow, row_len, HV)
    gate = heads[:, cut:]
    scores = jnp.einsum("rnd,rmd->rnm", queries, keys, preferred_element_type=F32)
    weights = (scores * decay).astype(BF16)
    mixed = jnp.einsum("rnm,rme->rne", weights, values, preferred_element_type=F32).reshape(-1, HV)
    centered = mixed - jnp.mean(mixed, axis=-1, keepdims=True)
    group_scale = lax.rsqrt(jnp.mean(centered * centered, axis=-1, keepdims=True) + GN_EPS)
    normed = centered * group_scale
    sig = jax.nn.sigmoid(gate)
    swish = gate * sig
    gated = (normed * swish).astype(BF16)
    x2 = xf + plane.scatter(lambda a: dot(a, w_o), gated, w_u)

    hat2, scale2 = normed_rows(x2)
    h2_parts, h2_blocks = plane.gather_parts(hat2.astype(BF16))
    acts, slopes = zip(*[gelu_and_slope(dot(a, w_u)) for a in h2_parts])
    act = plane.joined(acts)

    down_parts = dot_tn(act, dy).astype(BF16)
    down_rows = summed_along(down_parts)
    slope = plane.joined(lax.optimization_barrier((*slopes, down_parts))[:-1])
    d_hidden = (dot_nt(dy, w_d) * slope).astype(BF16)

    def up_product(held):
        return dot_tn(jnp.concatenate(held[:-1], axis=0), held[-1]).astype(BF16)

    t2, up_parts = plane.scatter(
        lambda a: dot_nt(a, w_u), d_hidden, late=(up_product, (*h2_blocks, d_hidden))
    )
    up_rows = summed_along(up_parts)
    d_x2 = cotangent[0].astype(F32) + norm_back(t2, hat2, scale2)
    d_branch_parts, d_branch_blocks = plane.gather_parts(after(d_x2.astype(BF16), down_rows))
    gate_slope = normed * sig * (1.0 + gate * (1.0 - sig))
    d_mixed, d_gate = [], []
    for part, at in zip(d_branch_parts, plane.parts_of(normed, swish, gate_slope, group_scale)):
        n_at, swish_at, slope_at, scale_at = at
        d_gated = dot_nt(part, w_o)
        d_gate.append((d_gated * slope_at).astype(BF16))
        d_mixed.append(norm_back(d_gated * swish_at, n_at, scale_at).astype(BF16))
    d_mixed, d_gate = plane.joined(d_mixed), plane.joined(d_gate)
    g_parts = dot_tn(h1, d_gate).astype(BF16)
    g_rows = summed_along(g_parts)
    d_mixed = after(d_mixed, g_parts)
    d_mixed = d_mixed.reshape(nrow, row_len, HV)
    d_values = jnp.einsum("rnm,rne->rme", weights, d_mixed, preferred_element_type=F32)
    d_values = d_values.astype(BF16).reshape(-1, HV)
    d_scores = jnp.einsum("rne,rme->rnm", d_mixed, values, preferred_element_type=F32)
    d_scores = (d_scores * decay).astype(BF16)
    d_query = jnp.einsum("rnm,rmd->rnd", d_scores, keys, preferred_element_type=F32)
    d_key = jnp.einsum("rnm,rnd->rmd", d_scores, queries, preferred_element_type=F32)
    d_query = unrotate(d_query, cosine, sine).astype(BF16)
    d_key = (unrotate(d_key, cosine, sine) * key_norm).astype(BF16)
    d_qkv = jnp.concatenate([d_query.reshape(-1, HK), d_key.reshape(-1, HK), d_values], axis=1)
    qkv_parts = dot_tn(h1, after(d_qkv, up_rows)).astype(BF16)
    qkv_rows = summed_along(qkv_parts)
    d_heads = jnp.concatenate([d_qkv, d_gate], axis=1)
    u1 = plane.scatter(
        lambda a: dot_nt(a, w_h), after(d_heads, up_rows)
    )
    tokens_grad = d_x2 + norm_back(u1, hat1, scale1)
    gated_last, *rest = lax.optimization_barrier((gated, *d_branch_blocks, qkv_parts))
    d_branch = jnp.concatenate(rest[:-1], axis=0)
    out_rows = plane.out_back(dot_tn(gated_last, d_branch).astype(BF16), u1)
    output = x2 + plane.scatter(lambda a: dot(a, w_d), after(act, tokens_grad))

    out_grad = out_rows.astype(F32)

    def by_rows(rows):
        return plane.exchange(rows.reshape(np_, width, -1)).astype(F32).transpose(1, 0, 2)

    up_sum = by_rows(after(up_rows, tokens_grad)).reshape(width, np_, nz, units).transpose(0, 2, 1, 3).reshape(width, -1)
    g_sum = by_rows(after(g_rows, tokens_grad)).reshape(width, -1)
    qkv_sum = by_rows(after(qkv_rows, output))
    q_sum = qkv_sum[:, :, :HK].reshape(width, -1)
    k_sum = qkv_sum[:, :, HK : 2 * HK].reshape(width, -1)
    v_sum = qkv_sum[:, :, 2 * HK :].reshape(width, -1)

    def gain_sum(pairs):
        return sum(jnp.sum(w.astype(F32) * g, axis=1) for w, g in pairs)

    gain1_grad = gain_sum([(w_query, q_sum), (w_key, k_sum), (w_value, v_sum), (w_gate, g_sum)])
    gain2_grad = gain_sum([(w_up, up_sum)])
    return (
        output.astype(BF16)[None],
        tokens_grad[None],
        gain1_grad,
        q_sum * gain_one,
        k_sum * gain_one,
        v_sum * gain_one,
        g_sum * gain_one,
        out_grad,
        gain2_grad,
        up_sum * gain_two,
        down_rows.astype(F32),
    )


def solution(mesh):
    batch, blocks = mesh.shape["batch"], mesh.shape["blk"]
    rows = HEADS // blocks
    split = Mesh(mesh.devices.reshape(batch // rows, rows, blocks), ALL)
    by_token = P(("z", "x"), "k", None)
    by_row = P(ALL, None)
    by_one = P(ALL)
    return jax.shard_map(
        shards,
        mesh=split,
        in_specs=(
            by_token,
            P(("z", "x"), None),
            by_one,
            by_row,
            by_row,
            by_row,
            by_row,
            by_row,
            by_one,
            by_row,
            by_row,
            by_token,
        ),
        out_specs=(
            by_token,
            by_token,
            by_one,
            by_row,
            by_row,
            by_row,
            by_row,
            by_row,
            by_one,
            by_row,
            by_row,
        ),
        check_vma=False,
    )
```
